32 devices in a mesh: dom: 2 (over x), space: 16 (over z, y, core).
Axes of the slice: x: 2, y: 2, z: 4, core: 2. Of those that a mesh axis runs over, the one named last changes fastest.
Arguments:
- inputs: bfloat16 [2, 32, 2048, 2048], P('dom', None, 'space'), parts along dimension 0, may hold values from -10.5 to 10.5
- target: bfloat16 [2, 32, 2048, 2048], P('dom', None, 'space'), parts along dimension 0, may hold values from -6 to 6
- spectral_weight: float32 [64, 32, 32, 128], P('space'), may hold values from -18 to 18
- local_weight: bfloat16 [32, 32], replicated, may hold values from -1 to 1
- bias_term: float32 [32], replicated, may hold values from -3 to 3
Outputs:
- grad_input: bfloat16 [2, 32, 2048, 2048], P('dom', None, 'space'), parts along dimension 0
- grad_spectral: float32 [64, 64, 32, 128], P('space', 'dom'), parts along dimension 1
- grad_local: float32 [64, 32], P('dom'), parts along dimension 0
- grad_bias: float32 [64], P('dom'), parts along dimension 0
The draws below stay inside these ranges and needn't reach their ends.
There are 2 independent parts, one for each index of `dom`. The reference program is written for one: setup_inputs(seed, part) draws one part's arguments, and reference() takes and returns one part's arrays. A program takes and returns all parts, laid end to end along the dimension named above; an argument that names none is the same for every part. Nothing has to cross between parts.
All inputs are finite; a program needn't handle non-finite values.
Results may differ from the reference program's by a relative error of at most 0.014.
Values may be sent and summed in bfloat16 or wider, within the bound.
A program may use at most 192 MiB of HBM per device.

```python
import math
import jax
import jax.numpy as jnp
from jax import lax

C = 32
H = 2048
W = 2048
KX = 64
KY = 64
STEPS = 1


def draw_inputs(key, part):
    row_place = jnp.arange(H, dtype=jnp.float32) / (H - 1) - 0.5
    noise_field = jax.random.truncated_normal(key, -6.0, 6.0, (STEPS, C, H, W), jnp.float32)
    factor = jnp.power(3.0, row_place)
    return (noise_field * factor[None, None, :, None]).astype(jnp.bfloat16)


def levels(rng, extent, pieces, low, high):
    gain = 1.0
    for dim, parts in pieces:
        heights = jax.random.uniform(jax.random.fold_in(jax.random.fold_in(rng, 6), dim), (parts,), jnp.float32, low / len(pieces), high / len(pieces))
        gain = gain * jnp.repeat(jnp.exp(heights), extent[dim] // parts).reshape((-1,) + (1,) * (len(extent) - 1 - dim))
    return gain


def centred(key, dims, width, bound, cuts=(), held_as=jnp.bfloat16):
    entries = jax.random.normal(key, dims, jnp.float32) * width
    if len(cuts) > 0:
        entries = levels(key, dims, cuts, -0.22, 0.18) * entries
    return jnp.clip(entries, min=-bound, max=bound).astype(held_as)


def setup_inputs(seed: int = 0, part: int = 0) -> dict:
    seeds = jax.random.split(jax.random.key(seed), 6)
    part_splits = jax.random.split(jax.random.fold_in(seeds[5], part), 6)
    inputs = draw_inputs(jax.random.fold_in(jax.random.fold_in(seeds[5], part), 71), part)
    target = centred(part_splits[1], (STEPS, C, H, W), 1.0, 6.0, ((2, 16),))
    spectral_weight = centred(seeds[2], (KY, C, C, 2 * KX), 3.0, 18.0, ((0, 16),), jnp.float32)
    local_weight = centred(seeds[3], (C, C), C ** -0.5, 1.0)
    bias_term = centred(seeds[4], (C,), 1.0, 3.0, (), jnp.float32)
    return dict(inputs=inputs, target=target, spectral_weight=spectral_weight, local_weight=local_weight, bias_term=bias_term)


PRECISE = lax.Precision.HIGHEST

def row_table():
    mode_index = jnp.arange(KY, dtype=jnp.int32)[:, None]
    column = jnp.arange(W, dtype=jnp.int32)[None, :]
    angles = (mode_index * column % W).astype(jnp.float32) * (2.0 * math.pi / W)
    factor = 1.0 / math.sqrt(H * W)
    return jnp.stack([jnp.cos(angles) * factor, -jnp.sin(angles) * factor]).astype(jnp.bfloat16)

def column_table(row_index):
    column = jnp.arange(KX, dtype=jnp.int32)
    frequency = jnp.where(column < KX // 2, column, column + H - KX)
    angles = (row_index[:, None] * frequency[None, :] % H).astype(jnp.float32) * (2.0 * math.pi / H)
    return jnp.concatenate([jnp.cos(angles), jnp.sin(angles)], axis=1)

def mode_weights(start_mode, mode_count):
    mode_index = start_mode + jnp.arange(mode_count, dtype=jnp.int32)
    return jnp.where(mode_index == 0, 1.0, 2.0).astype(jnp.float32)

def row_analysis(field_data, basis):
    return jnp.einsum('schw,pkw->kpsch', field_data.astype(jnp.float32), basis.astype(jnp.float32))

def row_synth(spectra, basis):
    return jnp.einsum('kpsch,pkw->schw', spectra.astype(jnp.float32), basis.astype(jnp.float32))

def column_modes(slab_part, basis):
    product = jnp.einsum('kpsch,hj->kpscj', slab_part, basis, precision=PRECISE)
    half_count = basis.shape[1] // 2
    real_part = product[:, 0, :, :, :half_count] + product[:, 1, :, :, half_count:]
    imag_part = product[:, 1, :, :, :half_count] - product[:, 0, :, :, half_count:]
    return jnp.concatenate([real_part, imag_part], axis=-1)

def column_synth(mode_data, basis):
    half_count = basis.shape[1] // 2
    real_part, imag_part = (mode_data[..., :half_count], mode_data[..., half_count:])
    cosines, sine_part = (basis[:, :half_count], basis[:, half_count:])
    first_part = jnp.einsum('ysok,hk->ysoh', real_part, cosines, precision=PRECISE) - jnp.einsum('ysok,hk->ysoh', imag_part, sine_part, precision=PRECISE)
    second = jnp.einsum('ysok,hk->ysoh', real_part, sine_part, precision=PRECISE) + jnp.einsum('ysok,hk->ysoh', imag_part, cosines, precision=PRECISE)
    return jnp.stack([first_part, second], axis=1).astype(jnp.bfloat16)

def split_complex(mode_data):
    half_count = mode_data.shape[-1] // 2
    return (mode_data[..., :half_count], mode_data[..., half_count:])

def mix_modes(input_modes, weight):
    spec_real, spec_imag = split_complex(input_modes)
    weight_real, weight_imag = split_complex(weight)
    form = 'ysck,ycok->ysok'
    out_real = jnp.einsum(form, spec_real, weight_real, precision=PRECISE) - jnp.einsum(form, spec_imag, weight_imag, precision=PRECISE)
    out_imag = jnp.einsum(form, spec_real, weight_imag, precision=PRECISE) + jnp.einsum(form, spec_imag, weight_real, precision=PRECISE)
    return jnp.concatenate([out_real, out_imag], axis=-1)

def mix_back(delta_modes, weight):
    delta_real, delta_imag = split_complex(delta_modes)
    weight_real, weight_imag = split_complex(weight)
    form = 'ysok,ycok->ysck'
    out_real = jnp.einsum(form, delta_real, weight_real, precision=PRECISE) + jnp.einsum(form, delta_imag, weight_imag, precision=PRECISE)
    out_imag = jnp.einsum(form, delta_imag, weight_real, precision=PRECISE) - jnp.einsum(form, delta_real, weight_imag, precision=PRECISE)
    return jnp.concatenate([out_real, out_imag], axis=-1)

def mix_grad(input_modes, delta_modes):
    spec_real, spec_imag = split_complex(input_modes)
    delta_real, delta_imag = split_complex(delta_modes)
    form = 'ysck,ysok->ycok'
    grad_real = jnp.einsum(form, spec_real, delta_real, precision=PRECISE) + jnp.einsum(form, spec_imag, delta_imag, precision=PRECISE)
    grad_imag = jnp.einsum(form, spec_real, delta_imag, precision=PRECISE) - jnp.einsum(form, spec_imag, delta_real, precision=PRECISE)
    return jnp.concatenate([grad_real, grad_imag], axis=-1)

def gelu_parts(value):
    normal_cdf = 0.5 * (1.0 + jax.scipy.special.erf(value * (1.0 / math.sqrt(2.0))))
    density = jnp.exp(-0.5 * value * value) * (1.0 / math.sqrt(2.0 * math.pi))
    return (value * normal_cdf, normal_cdf + value * density)

def reference(inputs, target, spectral_weight, local_weight, bias_term):
    row_basis = row_table()
    column_basis = column_table(jnp.arange(H, dtype=jnp.int32))
    mode_gain = mode_weights(0, KY)[:, None, None, None]
    input_modes = column_modes(row_analysis(inputs, row_basis), column_basis)
    mixed_modes = mix_modes(input_modes, spectral_weight) * mode_gain
    local_term = jnp.einsum('co,schw->sohw', local_weight.astype(jnp.float32), inputs.astype(jnp.float32))
    preact = row_synth(column_synth(mixed_modes, column_basis), row_basis) + local_term + bias_term[None, :, None, None]
    activated, derivative = gelu_parts(preact)
    delta_pre = ((activated - target.astype(jnp.float32)) * derivative).astype(jnp.bfloat16)
    delta_modes = column_modes(row_analysis(delta_pre, row_basis), column_basis) * mode_gain
    grad_spectral = mix_grad(input_modes, delta_modes)
    back_modes = mix_back(delta_modes, spectral_weight)
    back_local = jnp.einsum('co,sohw->schw', local_weight.astype(jnp.float32), delta_pre.astype(jnp.float32))
    grad_input = (row_synth(column_synth(back_modes, column_basis), row_basis) + back_local).astype(jnp.bfloat16)
    cell_count = STEPS * H * W
    grad_local = jnp.einsum('schw,sohw->co', inputs.astype(jnp.float32), delta_pre.astype(jnp.float32)) / cell_count
    grad_bias = lax.optimization_barrier(jnp.sum(delta_pre.astype(jnp.float32), axis=(0, 2, 3))) / cell_count
    return (grad_input, grad_spectral, grad_local, grad_bias)
```

```python
import functools
import math

import jax
import jax.numpy as jnp
from jax import lax
from jax.experimental import pallas as pl
from jax.experimental.pallas import tpu as pltpu
from jax.sharding import PartitionSpec as P

KX = 64
KY = 64
LIMIT = 56 * 1024 * 1024
F32 = jnp.float32
BF16 = jnp.bfloat16


def row_table(height, width):
    mode_index = jnp.arange(KY, dtype=jnp.int32)[:, None]
    column = jnp.arange(width, dtype=jnp.int32)[None, :]
    angles = (mode_index * column % width).astype(F32) * (2.0 * math.pi / width)
    factor = 1.0 / math.sqrt(height * width)
    return jnp.concatenate([jnp.cos(angles) * factor, -jnp.sin(angles) * factor]).astype(BF16)


def column_parts(row_index, height):
    column = jnp.arange(KX, dtype=jnp.int32)
    frequency = jnp.where(column < KX // 2, column, column + height - KX)
    angles = (row_index[:, None] * frequency[None, :] % height).astype(F32) * (2.0 * math.pi / height)
    return jnp.cos(angles), jnp.sin(angles)


def split_hi_lo(value):
    hi = value.astype(BF16)
    return hi, (value - hi.astype(F32)).astype(BF16)


def dot3(a, b_hi, b_lo):
    a_hi, a_lo = split_hi_lo(a)
    mm = functools.partial(jnp.dot, preferred_element_type=F32)
    return mm(a_hi, b_hi) + (mm(a_lo, b_hi) + mm(a_hi, b_lo))


def columns_of(row_modes, b_hi, b_lo):
    turned = row_modes.T
    half = turned.shape[0] // 2
    both = jnp.concatenate([turned[:half], turned[half:]], axis=1)
    return dot3(both, b_hi, b_lo)


def analysis_kernel(x_ref, bt_ref, bh_ref, bl_ref, out_ref):
    count, rows, width = x_ref.shape
    for c in range(count):
        row_modes = jnp.dot(x_ref[c], bt_ref[...], preferred_element_type=F32)
        out_ref[c] = columns_of(row_modes, bh_ref[...], bl_ref[...])


def analysis(x, bt, b_hi, b_lo):
    chans, rows, width = x.shape
    block = 4
    whole = lambda a: pl.BlockSpec(a.shape, lambda i: (0,) * a.ndim)
    return pl.pallas_call(
        analysis_kernel,
        grid=(chans // block,),
        in_specs=[pl.BlockSpec((block, rows, width), lambda i: (i, 0, 0)), whole(bt), whole(b_hi), whole(b_lo)],
        out_specs=pl.BlockSpec((block, KY, 2 * KX), lambda i: (i, 0, 0)),
        out_shape=jax.ShapeDtypeStruct((chans, KY, 2 * KX), F32),
        compiler_params=pltpu.CompilerParams(vmem_limit_bytes=LIMIT),
        name="analysis",
    )(x, bt, b_hi, b_lo)


def halves(value):
    half = value.shape[-1] // 2
    return value[..., :half], value[..., half:]


def cat(a, b):
    return jnp.concatenate([a, b], axis=-1)


def synth_columns(z, cb_hi, cb_lo, e_ref):
    re, im = halves(z)
    devices, _, _, rows = e_ref.shape
    both = jnp.concatenate([z, cat(im, -re)], axis=0)
    z_hi, z_lo = split_hi_lo(both)
    count = z.shape[0]
    step = max(rows, min(512, devices * rows))
    mm = functools.partial(jnp.dot, preferred_element_type=F32)
    for start in range(0, devices * rows, step):
        cols = pl.ds(start, step)
        e = mm(z_hi, cb_hi[:, cols]) + (mm(z_lo, cb_hi[:, cols]) + mm(z_hi, cb_lo[:, cols]))
        e = e.astype(BF16)
        for d in range(step // rows):
            for p in range(2):
                e_ref[start // rows + d, p] = e[p * count : (p + 1) * count, d * rows : (d + 1) * rows]


def mix_kernel(r_ref, w_ref, gain_ref, ch_ref, cl_ref, e_ref, x_ref):
    modes = w_ref.shape[0]
    parts = []
    for k in range(modes):
        x = r_ref[0, k]
        for s in range(1, r_ref.shape[0]):
            x = x + r_ref[s, k]
        x_ref[k] = x
        re, im = halves(x)
        x_rr, x_ii = cat(re, re), cat(-im, im)
        total = jnp.zeros(w_ref.shape[2:], F32)
        for c in range(w_ref.shape[1]):
            w = w_ref[k, c]
            wr, wi = halves(w)
            total = total + x_rr[c : c + 1] * w + x_ii[c : c + 1] * cat(wi, wr)
        parts.append(total * gain_ref[k])
    synth_columns(jnp.concatenate(parts, axis=0), ch_ref, cl_ref, e_ref)


def back_kernel(r_ref, w_ref, gain_ref, ch_ref, cl_ref, x_ref, e_ref, g_ref, back_ref):
    modes, chans = w_ref.shape[:2]
    for k in range(modes):
        d = r_ref[0, k]
        for s in range(1, r_ref.shape[0]):
            d = d + r_ref[s, k]
        d = d * gain_ref[k]
        dr, di = halves(d)
        d_sw = cat(di, dr)
        re, im = halves(x_ref[k])
        x_rr, x_ii = cat(re, re), cat(im, -im)
        for c in range(chans):
            g_ref[k, c] = x_rr[c : c + 1] * d + x_ii[c : c + 1] * d_sw
            wr, wi = halves(w_ref[k, c])
            term = d * cat(wr, wr) + d_sw * cat(wi, -wi)
            back_ref[pl.ds(k * chans + c, 1), :] = jnp.sum(term, axis=0, keepdims=True)
    synth_columns(back_ref[...], ch_ref, cl_ref, e_ref)


def gelu_delta(v, target):
    e = jnp.exp2(v * v * (-0.5 / math.log(2.0)))
    d = 1.0 + jnp.abs(v) * (0.3275911 / math.sqrt(2.0))
    t = pl.reciprocal(d, approx=True)
    t = t * (2.0 - d * t)
    a = (0.254829592, -0.284496736, 1.421413741, -1.453152027, 1.061405429)
    q = 0.5 * a[4]
    for coef in (a[3], a[2], a[1], a[0]):
        q = q * t + 0.5 * coef
    tail = q * t * e
    phi = jnp.where(v >= 0.0, 1.0 - tail, tail)
    slope = phi + v * e * (1.0 / math.sqrt(2.0 * math.pi))
    return (v * phi - target) * slope


def forward_kernel(x_ref, t_ref, e_ref, kron_ref, bias_ref, rb_ref, bt_ref, bh_ref, bl_ref,
                   delta_ref, modes_ref, weight_ref, rows_ref, acc_ref):
    step = pl.program_id(0)
    chans, rows, width = x_ref.shape
    flat = chans * rows
    tile = 512
    nt = (((1,), (1,)), ((), ()))

    @pl.when(step == 0)
    def _():
        acc_ref[...] = jnp.zeros_like(acc_ref)

    e = e_ref[...].reshape(flat, e_ref.shape[2])
    row_modes = jnp.zeros((flat, bt_ref.shape[1]), F32)
    for start in range(0, width, tile):
        cols = pl.ds(start, tile)
        x = x_ref[:, :, cols].reshape(flat, tile)
        v = jnp.dot(e, rb_ref[:, cols], preferred_element_type=F32)
        v = v + jnp.dot(kron_ref[...], x, preferred_element_type=F32) + bias_ref[...]
        target = t_ref[:, :, cols].reshape(flat, tile).astype(F32)
        delta = gelu_delta(v, target).astype(BF16)
        delta_ref[:, :, cols] = delta.reshape(chans, rows, tile)
        row_modes = row_modes + jnp.dot(delta, bt_ref[cols, :], preferred_element_type=F32)
        acc_ref[...] += lax.dot_general(x, delta, nt, preferred_element_type=F32)
    rows_ref[:, pl.ds(pl.multiple_of(step * rows, rows), rows), :] = row_modes.reshape(chans, rows, -1)

    @pl.when(step == pl.num_programs(0) - 1)
    def _():
        def body(o, carry):
            modes_ref[o] = columns_of(rows_ref[o], bh_ref[...], bl_ref[...])
            return carry

        lax.fori_loop(0, chans, body, 0)
        first = lax.broadcasted_iota(jnp.int32, (flat, flat), 0)
        second = lax.broadcasted_iota(jnp.int32, (flat, flat), 1)
        kept = jnp.where(first % rows == second % rows, acc_ref[...], 0.0)
        weight_ref[...] = jnp.sum(kept.reshape(chans, rows, flat), axis=1)


def forward(x, target, e, kron, bias, rb, bt, b_hi, b_lo, rows):
    chans, slab, width = x.shape
    flat = chans * rows
    whole = lambda a: pl.BlockSpec(a.shape, lambda i: (0,) * a.ndim)
    band = lambda last: pl.BlockSpec((chans, rows, last), lambda i: (0, i, 0))
    return pl.pallas_call(
        forward_kernel,
        grid=(slab // rows,),
        in_specs=[band(width), band(width), band(e.shape[2]), whole(kron), whole(bias), whole(rb), whole(bt),
                  whole(b_hi), whole(b_lo)],
        out_specs=[
            band(width),
            pl.BlockSpec((chans, KY, 2 * KX), lambda i: (0, 0, 0)),
            pl.BlockSpec((chans, flat), lambda i: (0, 0)),
        ],
        out_shape=[
            jax.ShapeDtypeStruct(x.shape, BF16),
            jax.ShapeDtypeStruct((chans, KY, 2 * KX), F32),
            jax.ShapeDtypeStruct((chans, flat), F32),
        ],
        scratch_shapes=[pltpu.VMEM((chans, slab, 2 * KY), F32), pltpu.VMEM((flat, flat), F32)],
        compiler_params=pltpu.CompilerParams(vmem_limit_bytes=LIMIT),
        name="forward",
    )(x, target, e, kron, bias, rb, bt, b_hi, b_lo)


def final_kernel(d_ref, e_ref, kron_ref, rb_ref, out_ref):
    chans, rows, width = d_ref.shape
    flat = chans * rows
    tile = 512
    e = e_ref[...].reshape(flat, e_ref.shape[2])
    for start in range(0, width, tile):
        cols = pl.ds(start, tile)
        v = jnp.dot(e, rb_ref[:, cols], preferred_element_type=F32)
        d = d_ref[:, :, cols].reshape(flat, tile)
        v = v + jnp.dot(kron_ref[...], d, preferred_element_type=F32)
        out_ref[:, :, cols] = v.astype(BF16).reshape(chans, rows, tile)


def final(delta, e, kron, rb, rows):
    chans, slab, width = delta.shape
    whole = lambda a: pl.BlockSpec(a.shape, lambda i: (0,) * a.ndim)
    band = lambda last: pl.BlockSpec((chans, rows, last), lambda i: (0, i, 0))
    return pl.pallas_call(
        final_kernel,
        grid=(slab // rows,),
        in_specs=[band(width), band(e.shape[2]), whole(kron), whole(rb)],
        out_specs=band(width),
        out_shape=jax.ShapeDtypeStruct(delta.shape, BF16),
        compiler_params=pltpu.CompilerParams(vmem_limit_bytes=LIMIT),
        name="final",
    )(delta, e, kron, rb)


def per_device(inputs, target, spectral_weight, local_weight, bias_term):
    samples, chans, slab, width = inputs.shape
    devices = lax.axis_size("space")
    height = slab * devices
    own = spectral_weight.shape[0]
    device = lax.axis_index("space")
    rows = 16

    rb = row_table(height, width)
    bt = rb.T
    rb_in = rb.reshape(2, devices, own, width).transpose(1, 0, 2, 3).reshape(2 * KY, width)
    cosines, sines = column_parts(device * slab + jnp.arange(slab, dtype=jnp.int32), height)
    b_hi, b_lo = split_hi_lo(
        jnp.concatenate([cat(cosines, -sines), cat(sines, cosines)], axis=0)
    )
    all_cos, all_sin = column_parts(jnp.arange(height, dtype=jnp.int32), height)
    c_hi, c_lo = split_hi_lo(cat(all_cos, -all_sin).T)
    mode = device * own + jnp.arange(own, dtype=jnp.int32)
    gain = jnp.broadcast_to(jnp.where(mode == 0, 1.0, 2.0).astype(F32)[:, None, None], (own, 1, 2 * KX))
    eye = jnp.eye(rows, dtype=BF16)
    kron_out = jnp.kron(local_weight.T, eye)
    kron_back = jnp.kron(local_weight, eye)
    bias = jnp.repeat(bias_term, rows)[:, None]
    params = pltpu.CompilerParams(vmem_limit_bytes=LIMIT)
    e_shape = jax.ShapeDtypeStruct((devices, 2, own * chans, slab), BF16)
    x_shape = jax.ShapeDtypeStruct((own, chans, 2 * KX), F32)

    def by_owner(modes):
        return modes.reshape(chans, devices, own, 2 * KX).transpose(1, 2, 0, 3).reshape(devices, -1)

    def to_rows(e):
        got = lax.all_to_all(e, "space", split_axis=0, concat_axis=0, tiled=True)
        got = got.reshape(devices * 2 * own, chans, slab)
        return got.transpose(1, 2, 0)

    x = inputs.reshape(chans, slab, width)
    modes = by_owner(analysis(x, bt, b_hi, b_lo))
    got = lax.all_to_all(modes, "space", split_axis=0, concat_axis=0, tiled=True)
    e, own_modes = pl.pallas_call(
        mix_kernel, out_shape=[e_shape, x_shape], compiler_params=params, name="mix"
    )(got.reshape(devices, own, chans, 2 * KX), spectral_weight, gain, c_hi, c_lo)

    delta, delta_modes, weight_part = forward(
        x, target.reshape(chans, slab, width), to_rows(e), kron_out, bias, rb_in, bt, b_hi, b_lo, rows
    )
    weight_part = weight_part.reshape(chans, chans, rows).sum(axis=-1)
    bias_part = delta_modes[:, 0, 0] * math.sqrt(height * width)
    extra = jnp.concatenate([weight_part.reshape(-1), bias_part, jnp.zeros((96,), F32)])
    extra = jnp.broadcast_to(extra[None], (devices, extra.shape[0]))
    sent = jnp.concatenate([by_owner(delta_modes), extra], axis=1)
    got = lax.all_to_all(sent, "space", split_axis=0, concat_axis=0, tiled=True)
    split = own * chans * 2 * KX
    e, grad_spectral = pl.pallas_call(
        back_kernel,
        out_shape=[e_shape, jax.ShapeDtypeStruct(spectral_weight.shape, F32)],
        scratch_shapes=[pltpu.VMEM((own * chans, 2 * KX), F32)],
        compiler_params=params,
        name="back",
    )(got[:, :split].reshape(devices, own, chans, 2 * KX), spectral_weight, gain, c_hi, c_lo, own_modes)
    totals = jnp.sum(got[:, split:], axis=0) / (samples * height * width)
    grad_local = totals[: chans * chans].reshape(chans, chans)
    grad_bias = totals[chans * chans : chans * chans + chans]
    grad_input = final(delta, to_rows(e), kron_back, rb_in, rows)
    return (grad_input.reshape(inputs.shape), grad_spectral, grad_local, grad_bias)


def solution(mesh):
    return jax.shard_map(
        per_device,
        mesh=mesh,
        in_specs=(
            P("dom", None, "space", None),
            P("dom", None, "space", None),
            P("space", None, None, None),
            P(),
            P(),
        ),
        out_specs=(
            P("dom", None, "space", None),
            P("space", "dom", None, None),
            P("dom", None),
            P("dom"),
        ),
        check_vma=False,
    )
```

```python
import functools
import math

import jax
import jax.numpy as jnp
import ml_dtypes
import numpy as np
from jax import lax
from jax.experimental import pallas as pl
from jax.experimental.pallas import tpu as pltpu
from jax.sharding import PartitionSpec as P

KX = 64
KY = 64
LIMIT = 56 * 1024 * 1024
F32 = jnp.float32
BF16 = jnp.bfloat16


def row_table(height, width):
    angles = (np.arange(KY)[:, None] * np.arange(width)[None, :] % width) * (2.0 * math.pi / width)
    factor = 1.0 / math.sqrt(height * width)
    return np.concatenate([np.cos(angles) * factor, -np.sin(angles) * factor]).astype(ml_dtypes.bfloat16)


def column_table(height):
    column = np.arange(KX)
    frequency = np.where(column < KX // 2, column, column + height - KX)
    angles = (frequency[:, None] * np.arange(height)[None, :] % height) * (2.0 * math.pi / height)
    table = np.concatenate([np.cos(angles), -np.sin(angles)]).astype(np.float32)
    hi = table.astype(ml_dtypes.bfloat16)
    return hi, (table - hi.astype(np.float32)).astype(ml_dtypes.bfloat16)


def spread(weight, rows):
    flat = weight.shape[0] * rows
    place = jnp.arange(flat, dtype=jnp.int32)
    chosen = (place[:, None] // rows == jnp.arange(weight.shape[0])[None, :]).astype(BF16)
    wide = jnp.dot(jnp.dot(chosen, weight), chosen.T)
    return jnp.where(place[:, None] % rows == place[None, :] % rows, wide, 0.0).astype(BF16)


def column_parts(row_index, height):
    column = jnp.arange(KX, dtype=jnp.int32)
    frequency = jnp.where(column < KX // 2, column, column + height - KX)
    angles = (row_index[:, None] * frequency[None, :] % height).astype(F32) * (2.0 * math.pi / height)
    return jnp.cos(angles), jnp.sin(angles)


def split_hi_lo(value):
    hi = value.astype(BF16)
    return hi, (value - hi.astype(F32)).astype(BF16)


def dot3(a, b_hi, b_lo):
    a_hi, a_lo = split_hi_lo(a)
    mm = functools.partial(jnp.dot, preferred_element_type=F32)
    return mm(a_hi, b_hi) + (mm(a_lo, b_hi) + mm(a_hi, b_lo))


def columns_of(row_modes, b_hi, b_lo):
    turned = row_modes.T
    half = turned.shape[0] // 2
    both = jnp.concatenate([turned[:half], turned[half:]], axis=1)
    return dot3(both, b_hi, b_lo)


def analysis_kernel(x_ref, bt_ref, bh_ref, bl_ref, out_ref):
    count, rows, width = x_ref.shape
    flat = x_ref[...].reshape(count * rows, width)
    row_modes = jnp.dot(flat, bt_ref[...], preferred_element_type=F32)
    for c in range(count):
        out_ref[c] = columns_of(row_modes[c * rows : (c + 1) * rows], bh_ref[...], bl_ref[...])


def analysis(x, bt, b_hi, b_lo):
    chans, rows, width = x.shape
    block = 4
    whole = lambda a: pl.BlockSpec(a.shape, lambda i: (0,) * a.ndim)
    return pl.pallas_call(
        analysis_kernel,
        grid=(chans // block,),
        in_specs=[pl.BlockSpec((block, rows, width), lambda i: (i, 0, 0)), whole(bt), whole(b_hi), whole(b_lo)],
        out_specs=pl.BlockSpec((block, KY, 2 * KX), lambda i: (i, 0, 0)),
        out_shape=jax.ShapeDtypeStruct((chans, KY, 2 * KX), F32),
        compiler_params=pltpu.CompilerParams(vmem_limit_bytes=LIMIT),
        name="analysis",
    )(x, bt, b_hi, b_lo)


def halves(value):
    half = value.shape[-1] // 2
    return value[..., :half], value[..., half:]


def cat(a, b):
    return jnp.concatenate([a, b], axis=-1)


def synth_columns(z, cb_hi, cb_lo, e_ref):
    re, im = halves(z)
    devices, _, _, rows = e_ref.shape
    both = jnp.concatenate([z, cat(im, -re)], axis=0)
    z_hi, z_lo = split_hi_lo(both)
    count = z.shape[0]
    step = max(rows, min(512, devices * rows))
    mm = functools.partial(jnp.dot, preferred_element_type=F32)
    for start in range(0, devices * rows, step):
        cols = pl.ds(start, step)
        e = mm(z_hi, cb_hi[:, cols]) + (mm(z_lo, cb_hi[:, cols]) + mm(z_hi, cb_lo[:, cols]))
        e = e.astype(BF16)
        for d in range(step // rows):
            for p in range(2):
                e_ref[start // rows + d, p] = e[p * count : (p + 1) * count, d * rows : (d + 1) * rows]


def mix_kernel(r_ref, w_ref, gain_ref, ch_ref, cl_ref, e_ref, x_ref):
    modes = w_ref.shape[0]
    parts = []
    for k in range(modes):
        x = r_ref[0, k]
        for s in range(1, r_ref.shape[0]):
            x = x + r_ref[s, k]
        x_ref[k] = x
        re, im = halves(x)
        x_rr, x_ii = cat(re, re), cat(-im, im)
        total = jnp.zeros(w_ref.shape[2:], F32)
        for c in range(w_ref.shape[1]):
            w = w_ref[k, c]
            wr, wi = halves(w)
            total = total + x_rr[c : c + 1] * w + x_ii[c : c + 1] * cat(wi, wr)
        parts.append(total * gain_ref[k])
    synth_columns(jnp.concatenate(parts, axis=0), ch_ref, cl_ref, e_ref)


def back_kernel(r_ref, w_ref, gain_ref, ch_ref, cl_ref, x_ref, e_ref, g_ref, back_ref):
    modes, chans = w_ref.shape[:2]
    for k in range(modes):
        d = r_ref[0, k]
        for s in range(1, r_ref.shape[0]):
            d = d + r_ref[s, k]
        d = d * gain_ref[k]
        dr, di = halves(d)
        d_sw = cat(di, dr)
        re, im = halves(x_ref[k])
        x_rr, x_ii = cat(re, re), cat(im, -im)
        for c in range(chans):
            g_ref[k, c] = x_rr[c : c + 1] * d + x_ii[c : c + 1] * d_sw
            wr, wi = halves(w_ref[k, c])
            term = d * cat(wr, wr) + d_sw * cat(wi, -wi)
            back_ref[pl.ds(k * chans + c, 1), :] = jnp.sum(term, axis=0, keepdims=True)
    synth_columns(back_ref[...], ch_ref, cl_ref, e_ref)


def gelu_delta(v, target):
    e = jnp.exp2(v * v * (-0.5 / math.log(2.0)))
    d = 1.0 + jnp.abs(v) * (0.3275911 / math.sqrt(2.0))
    t = pl.reciprocal(d, approx=True)
    t = t * (2.0 - d * t)
    a = (0.254829592, -0.284496736, 1.421413741, -1.453152027, 1.061405429)
    q = 0.5 * a[4]
    for coef in (a[3], a[2], a[1], a[0]):
        q = q * t + 0.5 * coef
    tail = q * t * e
    phi = jnp.where(v >= 0.0, 1.0 - tail, tail)
    slope = phi + v * e * (1.0 / math.sqrt(2.0 * math.pi))
    return (v * phi - target) * slope


def forward_kernel(x_ref, t_ref, e_ref, kron_ref, bias_ref, rb_ref, bt_ref, bh_ref, bl_ref,
                   delta_ref, modes_ref, weight_ref, rows_ref, acc_ref):
    step = pl.program_id(0)
    chans, rows, width = x_ref.shape
    flat = chans * rows
    tile = 512
    nt = (((1,), (1,)), ((), ()))

    @pl.when(step == 0)
    def _():
        acc_ref[...] = jnp.zeros_like(acc_ref)

    e = e_ref[...].reshape(flat, e_ref.shape[2])
    row_modes = jnp.zeros((flat, bt_ref.shape[1]), F32)
    for start in range(0, width, tile):
        cols = pl.ds(start, tile)
        x = x_ref[:, :, cols].reshape(flat, tile)
        v = jnp.dot(e, rb_ref[:, cols], preferred_element_type=F32)
        v = v + jnp.dot(kron_ref[...], x, preferred_element_type=F32) + bias_ref[...]
        target = t_ref[:, :, cols].reshape(flat, tile).astype(F32)
        delta = gelu_delta(v, target).astype(BF16)
        delta_ref[:, :, cols] = delta.reshape(chans, rows, tile)
        row_modes = row_modes + jnp.dot(delta, bt_ref[cols, :], preferred_element_type=F32)
        acc_ref[...] += lax.dot_general(x, delta, nt, preferred_element_type=F32)
    rows_ref[:, pl.ds(pl.multiple_of(step * rows, rows), rows), :] = row_modes.reshape(chans, rows, -1)

    @pl.when(step == pl.num_programs(0) - 1)
    def _():
        def body(o, carry):
            modes_ref[o] = columns_of(rows_ref[o], bh_ref[...], bl_ref[...])
            return carry

        lax.fori_loop(0, chans, body, 0)
        first = lax.broadcasted_iota(jnp.int32, (flat, flat), 0)
        second = lax.broadcasted_iota(jnp.int32, (flat, flat), 1)
        kept = jnp.where(first % rows == second % rows, acc_ref[...], 0.0)
        weight_ref[...] = jnp.sum(kept.reshape(chans, rows, flat), axis=1)


def forward(x, target, e, kron, bias, rb, bt, b_hi, b_lo, rows):
    chans, slab, width = x.shape
    flat = chans * rows
    whole = lambda a: pl.BlockSpec(a.shape, lambda i: (0,) * a.ndim)
    band = lambda last: pl.BlockSpec((chans, rows, last), lambda i: (0, i, 0))
    return pl.pallas_call(
        forward_kernel,
        grid=(slab // rows,),
        in_specs=[band(width), band(width), band(e.shape[2]), whole(kron), whole(bias), whole(rb), whole(bt),
                  whole(b_hi), whole(b_lo)],
        out_specs=[
            band(width),
            pl.BlockSpec((chans, KY, 2 * KX), lambda i: (0, 0, 0)),
            pl.BlockSpec((chans, flat), lambda i: (0, 0)),
        ],
        out_shape=[
            jax.ShapeDtypeStruct(x.shape, BF16),
            jax.ShapeDtypeStruct((chans, KY, 2 * KX), F32),
            jax.ShapeDtypeStruct((chans, flat), F32),
        ],
        scratch_shapes=[pltpu.VMEM((chans, slab, 2 * KY), F32), pltpu.VMEM((flat, flat), F32)],
        compiler_params=pltpu.CompilerParams(vmem_limit_bytes=LIMIT),
        name="forward",
    )(x, target, e, kron, bias, rb, bt, b_hi, b_lo)


def final_kernel(d_ref, e_ref, kron_ref, rb_ref, out_ref):
    chans, rows, width = d_ref.shape
    flat = chans * rows
    tile = 512
    e = e_ref[...].reshape(flat, e_ref.shape[2])
    for start in range(0, width, tile):
        cols = pl.ds(start, tile)
        v = jnp.dot(e, rb_ref[:, cols], preferred_element_type=F32)
        d = d_ref[:, :, cols].reshape(flat, tile)
        v = v + jnp.dot(kron_ref[...], d, preferred_element_type=F32)
        out_ref[:, :, cols] = v.astype(BF16).reshape(chans, rows, tile)


def final(delta, e, kron, rb, rows):
    chans, slab, width = delta.shape
    whole = lambda a: pl.BlockSpec(a.shape, lambda i: (0,) * a.ndim)
    band = lambda last: pl.BlockSpec((chans, rows, last), lambda i: (0, i, 0))
    return pl.pallas_call(
        final_kernel,
        grid=(slab // rows,),
        in_specs=[band(width), band(e.shape[2]), whole(kron), whole(rb)],
        out_specs=band(width),
        out_shape=jax.ShapeDtypeStruct(delta.shape, BF16),
        compiler_params=pltpu.CompilerParams(vmem_limit_bytes=LIMIT),
        name="final",
    )(delta, e, kron, rb)


def per_device(inputs, target, spectral_weight, local_weight, bias_term):
    samples, chans, slab, width = inputs.shape
    devices = lax.axis_size("space")
    height = slab * devices
    own = spectral_weight.shape[0]
    device = lax.axis_index("space")
    rows = 16

    rb = row_table(height, width)
    bt = jnp.asarray(np.ascontiguousarray(rb.T))
    rb_in = jnp.asarray(rb.reshape(2, devices, own, width).transpose(1, 0, 2, 3).reshape(2 * KY, width))
    cosines, sines = column_parts(device * slab + jnp.arange(slab, dtype=jnp.int32), height)
    b_hi, b_lo = split_hi_lo(
        jnp.concatenate([cat(cosines, -sines), cat(sines, cosines)], axis=0)
    )
    c_hi, c_lo = (jnp.asarray(table) for table in column_table(height))
    mode = device * own + jnp.arange(own, dtype=jnp.int32)
    gain = jnp.broadcast_to(jnp.where(mode == 0, 1.0, 2.0).astype(F32)[:, None, None], (own, 1, 2 * KX))
    kron_out = spread(local_weight.T, rows)
    kron_back = spread(local_weight, rows)
    bias = jnp.repeat(bias_term, rows)[:, None]
    params = pltpu.CompilerParams(vmem_limit_bytes=LIMIT)
    e_shape = jax.ShapeDtypeStruct((devices, 2, own * chans, slab), BF16)
    x_shape = jax.ShapeDtypeStruct((own, chans, 2 * KX), F32)

    def by_owner(modes):
        return modes.reshape(chans, devices, own, 2 * KX).transpose(1, 2, 0, 3).reshape(devices, -1)

    def to_rows(e):
        got = lax.all_to_all(e, "space", split_axis=0, concat_axis=0, tiled=True)
        got = got.reshape(devices * 2 * own, chans, slab)
        return got.transpose(1, 2, 0)

    x = inputs.reshape(chans, slab, width)
    modes = by_owner(analysis(x, bt, b_hi, b_lo))
    got = lax.all_to_all(modes, "space", split_axis=0, concat_axis=0, tiled=True)
    e, own_modes = pl.pallas_call(
        mix_kernel, out_shape=[e_shape, x_shape], compiler_params=params, name="mix"
    )(got.reshape(devices, own, chans, 2 * KX), spectral_weight, gain, c_hi, c_lo)

    delta, delta_modes, weight_part = forward(
        x, target.reshape(chans, slab, width), to_rows(e), kron_out, bias, rb_in, bt, b_hi, b_lo, rows
    )
    weight_part = weight_part.reshape(chans, chans, rows).sum(axis=-1)
    bias_part = delta_modes[:, 0, 0] * math.sqrt(height * width)
    extra = jnp.concatenate([weight_part.reshape(-1), bias_part, jnp.zeros((992,), F32)])
    extra = jnp.broadcast_to(extra[None], (devices, extra.shape[0]))
    got = lax.all_to_all(by_owner(delta_modes), "space", split_axis=0, concat_axis=0, tiled=True)
    terms = lax.all_to_all(extra, "space", split_axis=0, concat_axis=0, tiled=True)
    e, grad_spectral = pl.pallas_call(
        back_kernel,
        out_shape=[e_shape, jax.ShapeDtypeStruct(spectral_weight.shape, F32)],
        scratch_shapes=[pltpu.VMEM((own * chans, 2 * KX), F32)],
        compiler_params=params,
        name="back",
    )(got.reshape(devices, own, chans, 2 * KX), spectral_weight, gain, c_hi, c_lo, own_modes)
    totals = jnp.sum(terms, axis=0) / (samples * height * width)
    grad_local = totals[: chans * chans].reshape(chans, chans)
    grad_bias = totals[chans * chans : chans * chans + chans]
    grad_input = final(delta, to_rows(e), kron_back, rb_in, rows)
    return (grad_input.reshape(inputs.shape), grad_spectral, grad_local, grad_bias)


def solution(mesh):
    return jax.shard_map(
        per_device,
        mesh=mesh,
        in_specs=(
            P("dom", None, "space", None),
            P("dom", None, "space", None),
            P("space", None, None, None),
            P(),
            P(),
        ),
        out_specs=(
            P("dom", None, "space", None),
            P("space", "dom", None, None),
            P("dom", None),
            P("dom"),
        ),
        check_vma=False,
    )
```
